32 devices in a mesh: groups: 2 (over y), expert: 8 (over z, x), attn: 2 (over core).
Axes of the slice: x: 2, y: 2, z: 4, core: 2. Of those that a mesh axis runs over, the one named last changes fastest.
Arguments:
- tokens: bfloat16 [3, 512, 7168], P(None, ('groups', 'expert'), 'attn'), parts along dimension 1, may hold values from -6 to 6
- routes: int32 [3, 512, 8], P(None, ('groups', 'expert')), parts along dimension 1, may hold values from 0 to 255, all different within a row; in each aligned block of 32 rows (0 to 31, 32 to 63, ..., all dimensions but the last counted through in order) at most 2 rows name the same one
- route_weights: float32 [3, 512, 8], P(None, ('groups', 'expert')), parts along dimension 1, may hold values from 0.05 to 0.6
- gate_proj: bfloat16 [7168, 2048], P('attn', 'expert'), may hold values from -0.0625 to 0.0625
- up_proj: bfloat16 [7168, 2048], P('attn', 'expert'), may hold values from -0.0625 to 0.0625
- down_proj: bfloat16 [2048, 7168], P('expert', 'attn'), may hold values from -0.125 to 0.125
Outputs:
- mixed: bfloat16 [3, 512, 7168], P(None, ('groups', 'expert'), 'attn'), parts along dimension 1
The draws below stay inside these ranges and needn't reach their ends.
There are 2 independent parts, one for each index of `groups`. The reference program is written for one: setup_inputs(seed, part) draws one part's arguments, and reference() takes and returns one part's arrays. A program takes and returns all parts, laid end to end along the dimension named above; an argument that names none is the same for every part. Nothing has to cross between parts.
Inputs may be any that keep to these rules, and one draw needn't show every extreme that they name: `routes`: the 8 numbers of a row differ. In each aligned block of 32 rows (the rows of one device in one step) no expert is named by more than 2 rows, a bound that some block reaches.
All inputs are finite; a program needn't handle non-finite values.
Results may differ from the reference program's by a relative error of at most 0.0057.
Values may be sent and summed in bfloat16 or wider, within the bound.
No kernel may reach another device: no remote copies, remote signals or barrier semaphores. Data moves between devices by JAX's collectives and lax.ppermute only.
A program may use at most 64 MiB of HBM per device.

```python
import math
import jax
import jax.numpy as jnp
import numpy as np
from jax import lax

D = 7168
EF = 2048
NEXP = 256
TOPK = 8
STEPS = 3
ROWS_DEV = 32
GROUP = 8
HID_DEV = 256
EXP_FLIGHT = 1
CAP = 2
ROWS = 256
N_EXPERT = 8


def block_scale(own_key, shape, split, smallest, high):
    def one(axis_at, parts):
        heights = jax.random.uniform(jax.random.fold_in(jax.random.fold_in(own_key, 6), axis_at), (parts,), jnp.float32, smallest / len(split), high / len(split))
        return jnp.repeat(jnp.exp(heights), shape[axis_at] // parts).reshape((-1,) + (1,) * (len(shape) - axis_at - 1))

    factor_of = one(*split[0])
    for cut in split[1:]:
        factor_of = factor_of * one(*cut)
    return factor_of


def shared_out(stream_key, own, number, rows, number_of, top, most, skew):
    order = jax.random.permutation(stream_key, number_of)
    packed, usual = load_shares(number_of, rows * top, most, skew, True), load_shares(number_of, rows * top, most, skew, False)
    places = jnp.arange(number_of)

    def named(lengths, offset_by):
        used = int((lengths > 0).sum())
        fixed = max(1, used // 4)
        passed = fixed + (places - fixed + offset_by * (used - fixed)) % max(1, number_of - fixed)
        return jnp.zeros((number_of,), jnp.int32).at[order[jnp.where(places < fixed, places, passed)]].set(jnp.asarray(lengths, jnp.int32))

    lengths = jnp.where(number % 4 == 0, named(packed, number // 4), named(usual, number - number // 4 - 1))
    mixed = jax.random.permutation(jax.random.fold_in(own, 3), number_of)
    giver, receiver = mixed[0:number_of // 2 * 2:2], mixed[1:number_of // 2 * 2:2]
    slack = jnp.minimum(lengths[giver] - 1, most - lengths[receiver]) // 2
    slack = jnp.where((giver == order[0]) | (receiver == order[0]) | (lengths[receiver] == 0), 0, jnp.maximum(slack, 0))
    passed = jax.random.randint(jax.random.fold_in(own, 4), (number_of // 2,), 0, 1 << 20) % (slack + 1)
    lengths = lengths.at[giver].add(-passed).at[receiver].add(passed)
    labels = jnp.searchsorted(jnp.cumsum(lengths), jnp.arange(rows * top), side="right").astype(jnp.int32)
    grid = labels.reshape(top, rows).T
    grid = grid[jax.random.permutation(jax.random.fold_in(own, 1), rows)]
    offset_by = jax.random.randint(jax.random.fold_in(own, 2), (rows, 1), 0, top)
    return jnp.take_along_axis(grid, (jnp.arange(top)[None, :] + offset_by) % top, axis=1)


def load_shares(amount, total, most, lean, full):
    portions = [(1 << 20) // math.isqrt(standing ** lean) + 1 for standing in range(1, amount + 1)]
    largest = most if full else min(most, max(-(-total // amount), total * portions[0] // sum(portions)))
    least = 1 if total - largest >= amount - 1 else 0
    counts, surplus = [largest] + [least] * (amount - 1), total - largest - least * (amount - 1)
    while surplus > 0:
        movable = [i for i in range(1, amount) if counts[i] < largest] or [i for i in range(1, amount) if counts[i] < most]
        whole, remaining = sum([portions[i] for i in movable]), surplus
        for i in movable:
            extra = min(most - counts[i], max(1, remaining * portions[i] // whole), surplus)
            counts[i] = counts[i] + extra
            surplus = surplus - extra
    return np.array(counts)


def noise(own_key, shape, width, bound, split=(), held_as=jnp.bfloat16):
    level = block_scale(own_key, shape, split, -0.22, 0.18) if split else 1.0
    array = jax.random.normal(own_key, shape, jnp.float32) * width * level
    return jnp.minimum(jnp.maximum(array, -bound), bound).astype(held_as)


def setup_inputs(seed: int = 0, part: int = 0) -> dict:
    key_of = jax.random.split(jax.random.key(seed), 7)
    own_keys = jax.random.split(jax.random.fold_in(key_of[6], part), 7)
    tokens = noise(own_keys[0], (STEPS, ROWS, D), 1.0, 6.0, ((1, 8), (2, 2)))
    routes_keys = jax.random.split(jax.random.fold_in(own_keys[1], 1), STEPS * ROWS // ROWS_DEV)
    routes_turns = jax.random.permutation(jax.random.fold_in(own_keys[1], 3), STEPS * ROWS // ROWS_DEV)
    routes = jax.vmap(lambda own, number: shared_out(jax.random.fold_in(own_keys[1], 2), own, number, ROWS_DEV, NEXP, TOPK, CAP, 2))(routes_keys, routes_turns).reshape((STEPS, ROWS, TOPK))
    route_weights = jnp.clip(jnp.exp(math.log(0.6) - 2.4849067 * jax.random.uniform(own_keys[2], (STEPS, ROWS, TOPK), jnp.float32) ** block_scale(own_keys[2], (STEPS, ROWS, TOPK), ((1, 8),), -0.2, 0.2)), 0.05, 0.6)
    gate_proj = noise(key_of[3], (D, EXP_FLIGHT * EF), D ** -0.5, 0.0625, ((0, 2), (1, 8)))
    up_proj = noise(key_of[4], (D, EXP_FLIGHT * EF), D ** -0.5, 0.0625, ((0, 2), (1, 8)))
    down_proj = noise(key_of[5], (EXP_FLIGHT * EF, D), EF ** -0.5, 0.125, ((0, 8), (1, 2)))
    return {"tokens": tokens, "routes": routes, "route_weights": route_weights, "gate_proj": gate_proj, "up_proj": up_proj, "down_proj": down_proj}


def one_step(tokens, routes, route_weights, gate_proj, up_proj, down_proj):
    count = tokens.shape[0]
    slots = N_EXPERT * CAP
    mixed = jnp.zeros((count, D), jnp.float32)
    row_ids = jnp.arange(count, dtype=jnp.int32)
    for expert_id in range(EXP_FLIGHT):
        named = routes == expert_id
        member = jnp.any(named, axis=1)
        weight = jnp.sum(jnp.where(named, route_weights, 0.0), axis=1)
        blocked = member.reshape(N_EXPERT, ROWS_DEV).astype(jnp.int32)
        before = jnp.cumsum(blocked, axis=1) - blocked
        slot = (jnp.arange(N_EXPERT, dtype=jnp.int32)[:, None] * CAP + before).reshape(count)
        slot = jnp.where(member, slot, slots).astype(jnp.int32)
        row_of = jnp.zeros((slots + 1,), jnp.int32).at[slot].set(row_ids)[:slots]
        live = jnp.zeros((slots + 1,), jnp.float32).at[slot].set(member.astype(jnp.float32))[:slots]
        chosen = tokens[row_of]
        lo_col = expert_id * EF
        gate = jnp.dot(chosen, gate_proj[:, lo_col:lo_col + EF], preferred_element_type=jnp.float32)
        up = jnp.dot(chosen, up_proj[:, lo_col:lo_col + EF], preferred_element_type=jnp.float32)
        hidden = (jax.nn.silu(gate) * up).astype(jnp.bfloat16)
        summed = jnp.zeros((slots, D), jnp.float32)
        for slice_id in range(GROUP):
            lo_unit = slice_id * HID_DEV
            piece = jnp.dot(hidden[:, lo_unit:lo_unit + HID_DEV],
                            down_proj[lo_col + lo_unit:lo_col + lo_unit + HID_DEV],
                            preferred_element_type=jnp.float32)
            rounded = lax.optimization_barrier(piece.astype(jnp.bfloat16))
            summed = summed + rounded.astype(jnp.float32)
        factor = live * weight[row_of]
        mixed = mixed.at[row_of].add(factor[:, None] * summed)
    return mixed.astype(jnp.bfloat16)


def reference(tokens, routes, route_weights, gate_proj, up_proj, down_proj):
    outputs = [one_step(tokens[step], routes[step], route_weights[step], gate_proj, up_proj, down_proj)
               for step in range(STEPS)]
    return jnp.stack(outputs, axis=0)
```

```python
import functools

import jax
import jax.numpy as jnp
from jax import lax
from jax.experimental import pallas as pl
from jax.experimental.pallas import tpu as pltpu
from jax.sharding import PartitionSpec as P

EF = 2048
STEPS = 3
CAP = 2
SLOTS = STEPS * CAP
PACK = 8
PIECES = 3
VMEM_BYTES = 48 * 1024 * 1024
BF16 = jnp.bfloat16
F32 = jnp.float32


def call(kernel, out_shape, *args, flops=0, bytes_accessed=0):
    return pl.pallas_call(
        kernel,
        out_shape=out_shape,
        in_specs=[pl.BlockSpec(memory_space=pltpu.VMEM)] * len(args),
        out_specs=jax.tree.map(lambda _: pl.BlockSpec(memory_space=pltpu.VMEM), out_shape),
        compiler_params=pltpu.CompilerParams(vmem_limit_bytes=VMEM_BYTES),
        cost_estimate=pl.CostEstimate(flops=flops, bytes_accessed=bytes_accessed, transcendentals=0),
    )(*args)


def dot(a, b):
    return jnp.dot(a, b, preferred_element_type=F32)


def slots_of(routes, expert_id):
    rows = routes.shape[0]
    per_step = rows // STEPS
    member = jnp.sum((routes == expert_id).astype(F32), axis=1, keepdims=True)
    at = lax.broadcasted_iota(jnp.int32, (rows, rows), 0)
    other = lax.broadcasted_iota(jnp.int32, (rows, rows), 1)
    earlier = (other < at) & (other // per_step == at // per_step)
    spread = jnp.broadcast_to(member, (rows, 128)).astype(BF16)
    before = dot(earlier.astype(BF16), spread)[:, :1].astype(jnp.int32)
    step = lax.broadcasted_iota(jnp.int32, (rows, 1), 0) // per_step
    return member > 0.5, step * CAP + before


def picks(member, slot, columns):
    rows = member.shape[0]
    lane = lax.broadcasted_iota(jnp.int32, (rows, columns), 1) % PACK
    main = member & (slot == lane) & (lane < SLOTS)
    rest = [
        member & (((lane == SLOTS) & (slot == t)) | ((lane == SLOTS + 1) & (slot == PIECES + t)))
        for t in range(PIECES)
    ]
    return main, rest


def select_kernel(flight, tokens_ref, routes_ref, out_ref):
    routes = routes_ref[...]
    piece = tokens_ref.shape[1] // (PIECES + 1)
    mains, rests = [], [[] for _ in range(PIECES)]
    for k in range(flight):
        member, slot = slots_of(routes, k)
        main, rest = picks(member, slot, PACK)
        mains.append(main.astype(F32))
        for t in range(PIECES):
            rests[t].append(rest[t].astype(F32))
    main = jnp.concatenate(mains, axis=1).T.astype(BF16)
    rest = jnp.concatenate([a for t in rests for a in t], axis=1).T.astype(BF16)
    last = dot(rest, tokens_ref[:, PIECES * piece :])
    count = flight * PACK
    for t in range(PIECES):
        cols = slice(t * piece, (t + 1) * piece)
        out_ref[:, cols] = (
            dot(main, tokens_ref[:, cols]) + last[t * count : (t + 1) * count]
        ).astype(BF16)


def gate_up_kernel(own_ref, one_ref, two_ref, three_ref, gate_ref, up_ref, out_ref):
    packed = own_ref.shape[1]
    piece = packed // PIECES
    hidden = gate_ref.shape[1]
    x = jnp.concatenate([r[...] for r in (own_ref, one_ref, two_ref, three_ref)], axis=0)
    rows = x.shape[0]
    tall = jnp.concatenate([x[:, t * piece : (t + 1) * piece] for t in range(PIECES)], axis=0)
    place = lax.broadcasted_iota(jnp.int32, (rows, hidden), 0) % PACK
    for h, ref in enumerate((gate_ref, up_ref)):
        total = dot(x, ref[:packed, :])
        last = dot(tall, ref[packed:, :])
        for t in range(PIECES):
            part = last[t * rows : (t + 1) * rows]
            low = pltpu.roll(part, rows - (SLOTS - t), 0)
            high = pltpu.roll(part, rows - (SLOTS + 1 - PIECES - t), 0)
            total = total + jnp.where(place == t, low, 0.0) + jnp.where(place == PIECES + t, high, 0.0)
        out_ref[:, h * hidden : (h + 1) * hidden] = total


def down_kernel(mine_ref, peer_ref, down_ref, *out_refs):
    rows = mine_ref.shape[0]
    depth = down_ref.shape[0]
    piece = down_ref.shape[1] // (PIECES + 1)
    total = mine_ref[...] + peer_ref[...]
    gate, up = total[:, :depth], total[:, depth:]
    hidden = (gate / (1.0 + jnp.exp(-gate)) * up).astype(BF16).astype(F32)
    place = lax.broadcasted_iota(jnp.int32, (rows, depth), 0) % PACK
    main = jnp.where(place < SLOTS, hidden, 0.0).astype(BF16)
    tall = jnp.concatenate(
        [
            jnp.where(place == SLOTS, pltpu.roll(hidden, SLOTS - t, 0), 0.0)
            + jnp.where(place == SLOTS + 1, pltpu.roll(hidden, SLOTS + 1 - PIECES - t, 0), 0.0)
            for t in range(PIECES)
        ],
        axis=0,
    ).astype(BF16)
    last = dot(tall, down_ref[:, PIECES * piece :])
    count = rows // len(out_refs)
    for t in range(PIECES):
        cols = slice(t * piece, (t + 1) * piece)
        part = (dot(main, down_ref[:, cols]) + last[t * rows : (t + 1) * rows]).astype(BF16)
        for b, ref in enumerate(out_refs):
            ref[:, cols] = part[b * count : (b + 1) * count]


def mix_kernel(flight, kept_ref, came_ref, routes_ref, weights_ref, out_ref):
    rows = routes_ref.shape[0]
    packed = kept_ref.shape[1]
    piece = packed // PIECES
    routes, scale = routes_ref[...], weights_ref[...]
    value = kept_ref[...] + came_ref[...].astype(F32)
    upper = value.astype(BF16).astype(F32)
    lower = value - upper
    first, last = None, None
    for k in range(flight):
        member, slot = slots_of(routes, k)
        weight = jnp.sum(jnp.where(routes == k, scale, 0.0), axis=1, keepdims=True)
        main, rest = picks(member, slot, 2 * PACK)
        take = slice(k * PACK, (k + 1) * PACK)
        both = jnp.concatenate([upper[take], lower[take]], axis=0).astype(BF16)
        one = weight * dot(main.astype(BF16), both)
        two = dot(rest[0].astype(BF16), both[:, :piece])
        for t in range(1, PIECES):
            two = two + dot(rest[t].astype(BF16), both[:, t * piece : (t + 1) * piece])
        two = weight * two
        first = one if first is None else first + one
        last = two if last is None else last + two
    out_ref[:, :packed] = first.astype(BF16)
    out_ref[:, packed:] = last.astype(BF16)


def local(tokens, routes, route_weights, gate_proj, up_proj, down_proj):
    steps, per_step, half = tokens.shape
    hidden_dev = gate_proj.shape[1]
    group = EF // hidden_dev
    devices = lax.axis_size("expert")
    flight = devices // group
    rows = steps * per_step
    packed = half // (PIECES + 1) * PIECES
    shape = jax.ShapeDtypeStruct
    tokens = tokens.reshape(rows, half)
    routes = routes.reshape(rows, routes.shape[2])
    route_weights = route_weights.reshape(rows, route_weights.shape[2])

    def swap(x, mask):
        return lax.ppermute(x, "expert", [(i, i ^ mask) for i in range(devices)])

    def across(x):
        if flight == 1:
            return x
        places = [[p + group * b for b in range(flight)] for p in range(group)]
        return lax.all_to_all(x, "expert", 0, 0, axis_index_groups=places, tiled=True)

    count = flight * PACK
    sent = call(
        functools.partial(select_kernel, flight), shape((count, packed), BF16), tokens, routes
    )
    sent = across(sent)
    pair = jnp.concatenate([sent, swap(sent, 4)], axis=0)
    came = [swap(pair, mask) for mask in (1, 2, 3)]
    all_rows = 8 * count
    products = call(
        gate_up_kernel,
        shape((all_rows, 2 * hidden_dev), F32),
        pair,
        *came,
        gate_proj,
        up_proj,
    )
    other = lax.ppermute(products, "attn", [(0, 1), (1, 0)])
    parts = call(
        down_kernel, [shape((2 * count, packed), BF16)] * 4, products, other, down_proj
    )
    back = [swap(parts[mask], mask) for mask in (1, 2, 3)]
    summed = parts[0].astype(F32)
    for x in back:
        summed = summed + x.astype(F32)
    kept, away = summed[:count], summed[count:].astype(BF16)
    came_back = swap(away, 4)
    if flight > 1:
        kept = across((kept + came_back.astype(F32)).astype(BF16)).astype(F32)
        came_back = jnp.zeros_like(came_back)
    mixed = call(
        functools.partial(mix_kernel, flight),
        shape((rows, half), BF16),
        kept,
        came_back,
        routes,
        route_weights,
    )
    return mixed.reshape(steps, per_step, half)


def solution(mesh):
    in_specs = (
        P(None, ("groups", "expert"), "attn"),
        P(None, ("groups", "expert"), None),
        P(None, ("groups", "expert"), None),
        P("attn", "expert"),
        P("attn", "expert"),
        P("expert", "attn"),
    )
    out_specs = P(None, ("groups", "expert"), "attn")
    return jax.shard_map(local, mesh=mesh, in_specs=in_specs, out_specs=out_specs, check_vma=False)
```

```python
import functools

import jax
import jax.numpy as jnp
from jax import lax
from jax.experimental import pallas as pl
from jax.experimental.pallas import tpu as pltpu
from jax.sharding import PartitionSpec as P

EF = 2048
STEPS = 3
CAP = 2
SLOTS = STEPS * CAP
PACK = 8
PIECES = 3
QUAD = (3, 2, 1)
LOADS = 4
MIB = 1024 * 1024
VMEM_BYTES = 32 * MIB
BF16 = jnp.bfloat16
F32 = jnp.float32


def call(kernel, out_shape, *args, scratch=(), here=(), out_here=False, cost=0, room=VMEM_BYTES):
    vmem, hbm = pl.BlockSpec(memory_space=pltpu.VMEM), pl.BlockSpec(memory_space=pltpu.HBM)
    return pl.pallas_call(
        kernel,
        out_shape=out_shape,
        in_specs=[hbm if i in here else vmem for i in range(len(args))],
        out_specs=jax.tree.map(lambda _: hbm if out_here else vmem, out_shape),
        scratch_shapes=scratch,
        compiler_params=pltpu.CompilerParams(vmem_limit_bytes=room),
        cost_estimate=pl.CostEstimate(flops=0, bytes_accessed=cost, transcendentals=0),
    )(*args)


def dot(a, b):
    return jnp.dot(a, b, preferred_element_type=F32)


def slots_of(routes, expert_id, step):
    choices, rows = routes.shape
    member = jnp.max((routes == expert_id).astype(F32), axis=0, keepdims=True)
    other = lax.broadcasted_iota(jnp.int32, (rows, rows), 0)
    at = lax.broadcasted_iota(jnp.int32, (rows, rows), 1)
    spread = jnp.broadcast_to(member, (choices, rows)).astype(BF16)
    before = dot(spread, (other < at).astype(BF16))[:1].astype(jnp.int32)
    return member > 0.5, step * CAP + before


def pick_kernel(flight, routes_ref, out_ref):
    steps, _, rows = routes_ref.shape
    place = lax.broadcasted_iota(jnp.int32, (PACK, rows), 0)
    for s in range(steps):
        routes = routes_ref[s]
        picked = [[] for _ in range(PIECES + 1)]
        for k in range(flight):
            member, slot = slots_of(routes, k, s)
            picked[0].append((member & (slot == place)).astype(F32))
            for t in range(PIECES):
                of_six = (place == SLOTS) & (slot == t)
                of_seven = (place == SLOTS + 1) & (slot == PIECES + t)
                picked[t + 1].append((member & (of_six | of_seven)).astype(F32))
        out_ref[s] = jnp.concatenate([a for p in picked for a in p], axis=0).astype(BF16)


def select_kernel(tokens_ref, picks_ref, out_ref):
    steps, _, half = tokens_ref.shape
    piece = half // (PIECES + 1)
    count = out_ref.shape[0]
    last, parts = None, [None] * PIECES
    for s in range(steps):
        one = dot(picks_ref[s, count:], tokens_ref[s, :, PIECES * piece :])
        last = one if last is None else last + one
        for t in range(PIECES):
            one = dot(picks_ref[s, :count], tokens_ref[s, :, t * piece : (t + 1) * piece])
            parts[t] = one if parts[t] is None else parts[t] + one
    for t in range(PIECES):
        out_ref[:, t * piece : (t + 1) * piece] = (
            parts[t] + last[t * count : (t + 1) * count]
        ).astype(BF16)


def load_kernel(*refs):
    count = (len(refs) - 2) // 2
    mark_ref, sems = refs[-2:]
    copies = []
    for i in range(count):
        rows = refs[i].shape[0] // LOADS
        for j in range(LOADS):
            part = pl.ds(j * rows, rows)
            copies.append(
                pltpu.make_async_copy(
                    refs[i].at[part], refs[count + i].at[part], sems.at[i * LOADS + j]
                )
            )
    for copy in copies:
        copy.start()
    mark_ref[...] = jnp.zeros_like(mark_ref)
    for copy in copies:
        copy.wait()


def pair_kernel(own_ref, came_ref, mark_ref, out_ref):
    del mark_ref
    both = jnp.concatenate([own_ref[...].astype(F32), came_ref[...].astype(F32)], axis=0)
    out_ref[...] = both.astype(BF16)


def load(*arrays):
    return call(
        load_kernel,
        [jax.ShapeDtypeStruct(a.shape, a.dtype) for a in arrays]
        + [jax.ShapeDtypeStruct((8, 128), F32)],
        *arrays,
        scratch=[pltpu.SemaphoreType.DMA((LOADS * len(arrays),))],
        here=range(len(arrays)),
        cost=sum(2 * a.size * a.dtype.itemsize for a in arrays),
        room=50 * MIB,
    )


def plan_kernel(flight, routes_ref, weights_ref, out_ref):
    steps, _, rows = routes_ref.shape
    lane = lax.broadcasted_iota(jnp.int32, (4 * 2 * PACK, rows), 0)
    block, place = lane // (2 * PACK), lane % PACK
    rest = jnp.where(place == SLOTS, block - 1, jnp.where(place == SLOTS + 1, PIECES + block - 1, -1))
    wanted = jnp.where(block == 0, jnp.where(place < SLOTS, place, -1), rest)
    for s in range(steps):
        routes, scale = routes_ref[s], weights_ref[s]
        for k in range(flight):
            member, slot = slots_of(routes, k, s)
            take = (member & (slot == wanted)).astype(F32)
            weight = jnp.sum(jnp.where(routes == k, scale, 0.0), axis=0, keepdims=True)
            both = jnp.concatenate([take, jnp.broadcast_to(weight, take.shape)], axis=0)
            out_ref[k, s * rows : (s + 1) * rows, :] = both.T


def gate_up_kernel(own_ref, one_ref, two_ref, three_ref, gate_ref, up_ref, out_ref):
    packed = own_ref.shape[1]
    piece = packed // PIECES
    hidden = gate_ref.shape[1]
    x = jnp.concatenate([r[...] for r in (own_ref, one_ref, two_ref, three_ref)], axis=0)
    rows = x.shape[0]
    tall = jnp.concatenate([x[:, t * piece : (t + 1) * piece] for t in range(PIECES)], axis=0)
    place = lax.broadcasted_iota(jnp.int32, (rows, hidden), 0) % PACK
    for h, ref in enumerate((gate_ref, up_ref)):
        total = dot(x, ref[:packed, :])
        last = dot(tall, ref[packed:, :])
        for t in range(PIECES):
            part = last[t * rows : (t + 1) * rows]
            low = pltpu.roll(part, rows - (SLOTS - t), 0)
            high = pltpu.roll(part, rows - (SLOTS + 1 - PIECES - t), 0)
            total = total + jnp.where(place == t, low, 0.0) + jnp.where(place == PIECES + t, high, 0.0)
        out_ref[:, h * hidden : (h + 1) * hidden] = total


def down_kernel(mine_ref, peer_ref, down_ref, *out_refs):
    rows = mine_ref.shape[0]
    depth = down_ref.shape[0]
    piece = down_ref.shape[1] // (PIECES + 1)
    total = mine_ref[...] + peer_ref[...]
    gate, up = total[:, :depth], total[:, depth:]
    hidden = (gate / (1.0 + jnp.exp(-gate)) * up).astype(BF16).astype(F32)
    place = lax.broadcasted_iota(jnp.int32, (rows, depth), 0) % PACK
    main = jnp.where(place < SLOTS, hidden, 0.0).astype(BF16)
    tall = jnp.concatenate(
        [
            jnp.where(place == SLOTS, pltpu.roll(hidden, SLOTS - t, 0), 0.0)
            + jnp.where(place == SLOTS + 1, pltpu.roll(hidden, SLOTS + 1 - PIECES - t, 0), 0.0)
            for t in range(PIECES)
        ],
        axis=0,
    ).astype(BF16)
    last = dot(tall, down_ref[:, PIECES * piece :])
    count = rows // len(out_refs)
    for t in range(PIECES):
        cols = slice(t * piece, (t + 1) * piece)
        part = (dot(main, down_ref[:, cols]) + last[t * rows : (t + 1) * rows]).astype(BF16)
        for b, ref in enumerate(out_refs):
            ref[:, cols] = part[b * count : (b + 1) * count]


def mix_kernel(flight, kept_ref, came_ref, plan_ref, out_ref, held, sems):
    packed = kept_ref.shape[1]
    piece = packed // PIECES
    value = kept_ref[...] + came_ref[...].astype(F32)
    upper = value.astype(BF16).astype(F32)
    lower = value - upper
    total = [None] * (PIECES + 1)
    for k in range(flight):
        weight = plan_ref[k, :, 4 * 2 * PACK : 4 * 2 * PACK + 1]
        main = plan_ref[k, :, : 2 * PACK].astype(BF16)
        rest = plan_ref[k, :, 2 * PACK : 4 * 2 * PACK].astype(BF16)
        take = slice(k * PACK, (k + 1) * PACK)
        both = jnp.concatenate([upper[take], lower[take]], axis=0).astype(BF16)
        tall = jnp.concatenate(
            [both[:, t * piece : (t + 1) * piece] for t in range(PIECES)], axis=0
        )
        for t in range(PIECES + 1):
            if t < PIECES:
                one = weight * dot(main, both[:, t * piece : (t + 1) * piece])
            else:
                one = weight * dot(rest, tall)
            total[t] = one if total[t] is None else total[t] + one
    copies = []
    for t in range(PIECES + 1):
        cols = pl.ds(t * piece, piece)
        held[:, t * piece : (t + 1) * piece] = total[t].astype(BF16)
        copies.append(pltpu.make_async_copy(held.at[:, cols], out_ref.at[:, cols], sems.at[t]))
        copies[-1].start()
    for copy in copies:
        copy.wait()


def local(tokens, routes, route_weights, gate_proj, up_proj, down_proj):
    steps, per_step, half = tokens.shape
    hidden_dev = gate_proj.shape[1]
    group = EF // hidden_dev
    devices = lax.axis_size("expert")
    flight = devices // group
    rows = steps * per_step
    packed = half // (PIECES + 1) * PIECES
    shape = jax.ShapeDtypeStruct
    routes = jnp.transpose(routes, (0, 2, 1))
    route_weights = jnp.transpose(route_weights, (0, 2, 1))

    def swap(x, mask):
        return lax.ppermute(x, "expert", [(i, i ^ mask) for i in range(devices)])

    def across(x):
        if flight == 1:
            return x
        places = [[p + group * b for b in range(flight)] for p in range(group)]
        return lax.all_to_all(x, "expert", 0, 0, axis_index_groups=places, tiled=True)

    count = flight * PACK
    picks = call(
        functools.partial(pick_kernel, flight),
        shape((steps, (PIECES + 1) * count, per_step), BF16),
        routes,
    )
    sent = call(select_kernel, shape((count, packed), BF16), tokens, picks)
    sent = across(sent)
    gate_proj, up_proj, mark = load(gate_proj, up_proj)
    plan = call(
        functools.partial(plan_kernel, flight),
        shape((flight, rows, 128), F32),
        routes,
        route_weights,
    )
    pair = call(pair_kernel, shape((2 * count, packed), BF16), sent, swap(sent, 4), mark)
    came = [swap(pair, mask) for mask in QUAD]
    all_rows = 8 * count
    products = call(
        gate_up_kernel,
        shape((all_rows, 2 * hidden_dev), F32),
        pair,
        *came,
        gate_proj,
        up_proj,
    )
    other = lax.ppermute(products, "attn", [(0, 1), (1, 0)])
    parts = call(
        down_kernel, [shape((2 * count, packed), BF16)] * 4, products, other, down_proj
    )
    back = [swap(part, mask) for part, mask in zip(parts[1:], QUAD)]
    summed = parts[0].astype(F32)
    for x in back:
        summed = summed + x.astype(F32)
    kept, away = summed[:count], summed[count:].astype(BF16)
    came_back = swap(away, 4)
    if flight > 1:
        kept = across((kept + came_back.astype(F32)).astype(BF16)).astype(F32)
        came_back = jnp.zeros_like(came_back)
    mixed = call(
        functools.partial(mix_kernel, flight),
        shape((rows, half), BF16),
        kept,
        came_back,
        plan,
        scratch=[pltpu.VMEM((rows, half), BF16), pltpu.SemaphoreType.DMA((PIECES + 1,))],
        out_here=True,
    )
    return mixed.reshape(steps, per_step, half)


def solution(mesh):
    in_specs = (
        P(None, ("groups", "expert"), "attn"),
        P(None, ("groups", "expert"), None),
        P(None, ("groups", "expert"), None),
        P("attn", "expert"),
        P("attn", "expert"),
        P("expert", "attn"),
    )
    out_specs = P(None, ("groups", "expert"), "attn")
    return jax.shard_map(local, mesh=mesh, in_specs=in_specs, out_specs=out_specs, check_vma=False)
```

```python
import functools

import jax
import jax.numpy as jnp
from jax import lax
from jax.experimental import pallas as pl
from jax.experimental.pallas import tpu as pltpu
from jax.sharding import PartitionSpec as P

EF = 2048
STEPS = 3
CAP = 2
SLOTS = STEPS * CAP
PACK = 8
PIECES = 3
SENT = 7
QUAD = (3, 2, 1)
LOADS = 4
MIB = 1024 * 1024
VMEM_BYTES = 32 * MIB
BF16 = jnp.bfloat16
F32 = jnp.float32


def call(kernel, out_shape, *args, scratch=(), here=(), out_here=False, cost=0, room=VMEM_BYTES):
    vmem, hbm = pl.BlockSpec(memory_space=pltpu.VMEM), pl.BlockSpec(memory_space=pltpu.HBM)
    return pl.pallas_call(
        kernel,
        out_shape=out_shape,
        in_specs=[hbm if i in here else vmem for i in range(len(args))],
        out_specs=jax.tree.map(lambda _: hbm if out_here else vmem, out_shape),
        scratch_shapes=scratch,
        compiler_params=pltpu.CompilerParams(vmem_limit_bytes=room),
        cost_estimate=pl.CostEstimate(flops=0, bytes_accessed=cost, transcendentals=0),
    )(*args)


def dot(a, b):
    return jnp.dot(a, b, preferred_element_type=F32)


def slots_of(routes, expert_id, step):
    choices, rows = routes.shape
    member = jnp.max((routes == expert_id).astype(F32), axis=0, keepdims=True)
    other = lax.broadcasted_iota(jnp.int32, (rows, rows), 0)
    at = lax.broadcasted_iota(jnp.int32, (rows, rows), 1)
    spread = jnp.broadcast_to(member, (choices, rows)).astype(BF16)
    before = dot(spread, (other < at).astype(BF16))[:1].astype(jnp.int32)
    return member > 0.5, step * CAP + before


def select_kernel(flight, tokens_ref, routes_ref, *refs):
    out_refs, (held, chosen, sems) = refs[:-3], refs[-3:]
    steps, rows, half = tokens_ref.shape
    piece = half // (PIECES + 1)
    copies = [
        pltpu.make_async_copy(tokens_ref.at[s], held.at[s], sems.at[s]) for s in range(steps)
    ]
    routes_copy = pltpu.make_async_copy(routes_ref, chosen, sems.at[steps])
    routes_copy.start()
    for copy in copies:
        copy.start()
    routes_copy.wait()
    place = lax.broadcasted_iota(jnp.int32, (PACK, rows), 0)
    mains, rests = [], []
    for s in range(steps):
        routes = chosen[s]
        main, rest = [], [[] for _ in range(PIECES)]
        for k in range(flight):
            member, slot = slots_of(routes, k, s)
            main.append((member & (slot == place)).astype(BF16))
            for t in range(PIECES):
                of_six = (place == SLOTS) & (slot == t)
                of_seven = (place == SLOTS + 1) & (slot == PIECES + t)
                rest[t].append((member & (of_six | of_seven)).astype(BF16))
        mains.append(jnp.concatenate(main, axis=0))
        rests.append(jnp.concatenate([a for t in rest for a in t], axis=0))
    count = flight * PACK
    last, parts = None, [None] * PIECES
    for s in range(steps):
        copies[s].wait()
        one = dot(rests[s], held[s, :, PIECES * piece :])
        last = one if last is None else last + one
        for t in range(PIECES):
            one = dot(mains[s], held[s, :, t * piece : (t + 1) * piece])
            parts[t] = one if parts[t] is None else parts[t] + one
    whole = jnp.concatenate(
        [parts[t] + last[t * count : (t + 1) * count] for t in range(PIECES)], axis=1
    ).astype(BF16)
    start = 0
    for ref in out_refs:
        ref[...] = whole[:, start : start + ref.shape[1]]
        start += ref.shape[1]


def load_kernel(*refs):
    count = (len(refs) - 2) // 2
    mark_ref, sems = refs[-2:]
    copies = []
    for i in range(count):
        rows = refs[i].shape[0] // LOADS
        for j in range(LOADS):
            part = pl.ds(j * rows, rows)
            copies.append(
                pltpu.make_async_copy(
                    refs[i].at[part], refs[count + i].at[part], sems.at[i * LOADS + j]
                )
            )
    for copy in copies:
        copy.start()
    mark_ref[...] = jnp.zeros_like(mark_ref)
    for copy in copies:
        copy.wait()


def pair_kernel(own_ref, came_ref, mark_ref, out_ref):
    del mark_ref
    both = jnp.concatenate([own_ref[...].astype(F32), came_ref[...].astype(F32)], axis=0)
    out_ref[...] = both.astype(BF16)


def load(*arrays):
    return call(
        load_kernel,
        [jax.ShapeDtypeStruct(a.shape, a.dtype) for a in arrays]
        + [jax.ShapeDtypeStruct((8, 128), F32)],
        *arrays,
        scratch=[pltpu.SemaphoreType.DMA((LOADS * len(arrays),))],
        here=range(len(arrays)),
        cost=sum(2 * a.size * a.dtype.itemsize for a in arrays),
        room=50 * MIB,
    )


def plan_kernel(flight, routes_hbm, weights_hbm, out_ref, routes_ref, weights_ref, sems):
    steps, _, rows = routes_ref.shape
    copies = [
        pltpu.make_async_copy(routes_hbm, routes_ref, sems.at[0]),
        pltpu.make_async_copy(weights_hbm, weights_ref, sems.at[1]),
    ]
    for copy in copies:
        copy.start()
    for copy in copies:
        copy.wait()
    lane = lax.broadcasted_iota(jnp.int32, (4 * 2 * PACK, rows), 0)
    block, place = lane // (2 * PACK), lane % PACK
    rest = jnp.where(place == SLOTS, block - 1, jnp.where(place == SLOTS + 1, PIECES + block - 1, -1))
    wanted = jnp.where(block == 0, jnp.where(place < SLOTS, place, -1), rest)
    for s in range(steps):
        routes, scale = routes_ref[s], weights_ref[s]
        for k in range(flight):
            member, slot = slots_of(routes, k, s)
            take = (member & (slot == wanted)).astype(F32)
            weight = jnp.sum(jnp.where(routes == k, scale, 0.0), axis=0, keepdims=True)
            both = jnp.concatenate([take, jnp.broadcast_to(weight, take.shape)], axis=0)
            out_ref[k, s * rows : (s + 1) * rows, :] = both.T


def gate_up_kernel(own_ref, one_ref, two_ref, three_ref, gate_ref, up_ref, out_ref):
    packed = own_ref.shape[1]
    piece = packed // PIECES
    hidden = gate_ref.shape[1]
    x = jnp.concatenate([r[...] for r in (own_ref, one_ref, two_ref, three_ref)], axis=0)
    rows = x.shape[0]
    tall = jnp.concatenate([x[:, t * piece : (t + 1) * piece] for t in range(PIECES)], axis=0)
    place = lax.broadcasted_iota(jnp.int32, (rows, hidden), 0) % PACK
    for h, ref in enumerate((gate_ref, up_ref)):
        total = dot(x, ref[:packed, :])
        last = dot(tall, ref[packed:, :])
        for t in range(PIECES):
            part = last[t * rows : (t + 1) * rows]
            low = pltpu.roll(part, rows - (SLOTS - t), 0)
            high = pltpu.roll(part, rows - (SLOTS + 1 - PIECES - t), 0)
            total = total + jnp.where(place == t, low, 0.0) + jnp.where(place == PIECES + t, high, 0.0)
        out_ref[:, h * hidden : (h + 1) * hidden] = total


def down_kernel(mine_ref, peer_ref, down_ref, *out_refs):
    rows = mine_ref.shape[0]
    depth = down_ref.shape[0]
    piece = down_ref.shape[1] // (PIECES + 1)
    total = mine_ref[...] + peer_ref[...]
    gate, up = total[:, :depth], total[:, depth:]
    hidden = (gate / (1.0 + jnp.exp(-gate)) * up).astype(BF16).astype(F32)
    place = lax.broadcasted_iota(jnp.int32, (rows, depth), 0) % PACK
    main = jnp.where(place < SLOTS, hidden, 0.0).astype(BF16)
    tall = jnp.concatenate(
        [
            jnp.where(place == SLOTS, pltpu.roll(hidden, SLOTS - t, 0), 0.0)
            + jnp.where(place == SLOTS + 1, pltpu.roll(hidden, SLOTS + 1 - PIECES - t, 0), 0.0)
            for t in range(PIECES)
        ],
        axis=0,
    ).astype(BF16)
    last = dot(tall, down_ref[:, PIECES * piece :])
    count = rows // len(out_refs)
    for t in range(PIECES):
        cols = slice(t * piece, (t + 1) * piece)
        part = (dot(main, down_ref[:, cols]) + last[t * rows : (t + 1) * rows]).astype(BF16)
        for b, ref in enumerate(out_refs):
            ref[:, cols] = part[b * count : (b + 1) * count]


def mix_kernel(flight, kept_ref, came_ref, plan_ref, out_ref, held, sems):
    packed = kept_ref.shape[1]
    piece = packed // PIECES
    value = kept_ref[...] + came_ref[...].astype(F32)
    upper = value.astype(BF16).astype(F32)
    lower = value - upper
    total = [None] * (PIECES + 1)
    for k in range(flight):
        weight = plan_ref[k, :, 4 * 2 * PACK : 4 * 2 * PACK + 1]
        main = plan_ref[k, :, : 2 * PACK].astype(BF16)
        rest = plan_ref[k, :, 2 * PACK : 4 * 2 * PACK].astype(BF16)
        take = slice(k * PACK, (k + 1) * PACK)
        both = jnp.concatenate([upper[take], lower[take]], axis=0).astype(BF16)
        tall = jnp.concatenate(
            [both[:, t * piece : (t + 1) * piece] for t in range(PIECES)], axis=0
        )
        for t in range(PIECES + 1):
            if t < PIECES:
                one = weight * dot(main, both[:, t * piece : (t + 1) * piece])
            else:
                one = weight * dot(rest, tall)
            total[t] = one if total[t] is None else total[t] + one
    copies = []
    for t in range(PIECES + 1):
        cols = pl.ds(t * piece, piece)
        held[:, t * piece : (t + 1) * piece] = total[t].astype(BF16)
        copies.append(pltpu.make_async_copy(held.at[:, cols], out_ref.at[:, cols], sems.at[t]))
        copies[-1].start()
    for copy in copies:
        copy.wait()


def local(tokens, routes, route_weights, gate_proj, up_proj, down_proj):
    steps, per_step, half = tokens.shape
    hidden_dev = gate_proj.shape[1]
    group = EF // hidden_dev
    devices = lax.axis_size("expert")
    flight = devices // group
    rows = steps * per_step
    packed = half // (PIECES + 1) * PIECES
    shape = jax.ShapeDtypeStruct
    routes = jnp.transpose(routes, (0, 2, 1))
    route_weights = jnp.transpose(route_weights, (0, 2, 1))

    def swap(x, mask):
        return lax.ppermute(x, "expert", [(i, i ^ mask) for i in range(devices)])

    def across(x):
        if flight == 1:
            return x
        places = [[p + group * b for b in range(flight)] for p in range(group)]
        return lax.all_to_all(x, "expert", 0, 0, axis_index_groups=places, tiled=True)

    count = flight * PACK
    sent = call(
        functools.partial(select_kernel, flight),
        [shape((count, packed // SENT), BF16)] * SENT,
        tokens,
        routes,
        scratch=[
            pltpu.VMEM(tokens.shape, BF16),
            pltpu.VMEM(routes.shape, jnp.int32),
            pltpu.SemaphoreType.DMA((steps + 1,)),
        ],
        here=(0, 1),
        room=55169 * 1024,
    )
    sent = across(jnp.concatenate(sent, axis=1))
    gate_proj, up_proj, mark = load(gate_proj, up_proj)
    plan = call(
        functools.partial(plan_kernel, flight),
        shape((flight, rows, 128), F32),
        routes,
        route_weights,
        scratch=[
            pltpu.VMEM(routes.shape, jnp.int32),
            pltpu.VMEM(route_weights.shape, F32),
            pltpu.SemaphoreType.DMA((2,)),
        ],
        here=(0, 1),
    )
    high = [bit for bit in (group >> n for n in range(1, group.bit_length())) if bit >= 4]
    block = sent
    for bit in high:
        block = call(
            pair_kernel,
            shape((2 * block.shape[0], packed), BF16),
            block,
            swap(block, bit),
            mark,
        )
    came = [swap(block, mask) for mask in QUAD]
    products = call(
        gate_up_kernel,
        shape((group * count, 2 * hidden_dev), F32),
        block,
        *came,
        gate_proj,
        up_proj,
    )
    other = lax.ppermute(products, "attn", [(0, 1), (1, 0)])
    parts = call(down_kernel, [shape(block.shape, BF16)] * 4, products, other, down_proj)
    back = [swap(part, mask) for part, mask in zip(parts[1:], QUAD)]
    summed = parts[0].astype(F32)
    for x in back:
        summed = summed + x.astype(F32)
    for bit in reversed(high):
        half_rows = summed.shape[0] // 2
        kept, away = summed[:half_rows], summed[half_rows:].astype(BF16)
        came_back = swap(away, bit)
        summed = kept + came_back.astype(F32)
    if flight > 1:
        kept = across(summed.astype(BF16)).astype(F32)
        came_back = jnp.zeros(kept.shape, BF16)
    mixed = call(
        functools.partial(mix_kernel, flight),
        shape((rows, half), BF16),
        kept,
        came_back,
        plan,
        scratch=[pltpu.VMEM((rows, half), BF16), pltpu.SemaphoreType.DMA((PIECES + 1,))],
        out_here=True,
    )
    return mixed.reshape(steps, per_step, half)


def solution(mesh):
    in_specs = (
        P(None, ("groups", "expert"), "attn"),
        P(None, ("groups", "expert"), None),
        P(None, ("groups", "expert"), None),
        P("attn", "expert"),
        P("attn", "expert"),
        P("expert", "attn"),
    )
    out_specs = P(None, ("groups", "expert"), "attn")
    return jax.shard_map(local, mesh=mesh, in_specs=in_specs, out_specs=out_specs, check_vma=False)
```

```python
import functools

import jax
import jax.numpy as jnp
from jax import lax
from jax.experimental import pallas as pl
from jax.experimental.pallas import tpu as pltpu
from jax.sharding import PartitionSpec as P

EF = 2048
STEPS = 3
CAP = 2
SLOTS = STEPS * CAP
PACK = 8
PIECES = 3
SENT = 7
QUAD = (3, 2, 1)
LOADS = 4
MIB = 1024 * 1024
VMEM_BYTES = 32 * MIB
BF16 = jnp.bfloat16
F32 = jnp.float32


def call(kernel, out_shape, *args, scratch=(), here=(), out_here=False, cost=0, room=VMEM_BYTES):
    vmem, hbm = pl.BlockSpec(memory_space=pltpu.VMEM), pl.BlockSpec(memory_space=pltpu.HBM)
    return pl.pallas_call(
        kernel,
        out_shape=out_shape,
        in_specs=[hbm if i in here else vmem for i in range(len(args))],
        out_specs=jax.tree.map(lambda _: hbm if out_here else vmem, out_shape),
        scratch_shapes=scratch,
        compiler_params=pltpu.CompilerParams(vmem_limit_bytes=room),
        cost_estimate=pl.CostEstimate(flops=0, bytes_accessed=cost, transcendentals=0),
    )(*args)


def dot(a, b):
    return jnp.dot(a, b, preferred_element_type=F32)


def slots_of(routes, expert_id, step):
    choices, rows = routes.shape
    member = jnp.max((routes == expert_id).astype(F32), axis=0, keepdims=True)
    other = lax.broadcasted_iota(jnp.int32, (rows, rows), 0)
    at = lax.broadcasted_iota(jnp.int32, (rows, rows), 1)
    spread = jnp.broadcast_to(member, (choices, rows)).astype(BF16)
    before = dot(spread, (other < at).astype(BF16))[:1].astype(jnp.int32)
    return member > 0.5, step * CAP + before


def select_kernel(flight, tokens_ref, routes_ref, *refs):
    out_refs, (held, chosen, sems) = refs[:-3], refs[-3:]
    steps, rows, half = tokens_ref.shape
    piece = half // (PIECES + 1)
    copies = [
        pltpu.make_async_copy(tokens_ref.at[s], held.at[s], sems.at[s]) for s in range(steps)
    ]
    routes_copy = pltpu.make_async_copy(routes_ref, chosen, sems.at[steps])
    routes_copy.start()
    for copy in copies:
        copy.start()
    routes_copy.wait()
    place = lax.broadcasted_iota(jnp.int32, (PACK, rows), 0)
    mains, rests = [], []
    for s in range(steps):
        routes = chosen[s]
        main, rest = [], [[] for _ in range(PIECES)]
        for k in range(flight):
            member, slot = slots_of(routes, k, s)
            main.append((member & (slot == place)).astype(BF16))
            for t in range(PIECES):
                of_six = (place == SLOTS) & (slot == t)
                of_seven = (place == SLOTS + 1) & (slot == PIECES + t)
                rest[t].append((member & (of_six | of_seven)).astype(BF16))
        mains.append(jnp.concatenate(main, axis=0))
        rests.append(jnp.concatenate([a for t in rest for a in t], axis=0))
    count = flight * PACK
    last, parts = None, [None] * PIECES
    for s in range(steps):
        copies[s].wait()
        one = dot(rests[s], held[s, :, PIECES * piece :])
        last = one if last is None else last + one
        for t in range(PIECES):
            one = dot(mains[s], held[s, :, t * piece : (t + 1) * piece])
            parts[t] = one if parts[t] is None else parts[t] + one
    whole = jnp.concatenate(
        [parts[t] + last[t * count : (t + 1) * count] for t in range(PIECES)], axis=1
    ).astype(BF16)
    start = 0
    for ref in out_refs:
        ref[...] = whole[:, start : start + ref.shape[1]]
        start += ref.shape[1]


def load_kernel(*refs):
    count = (len(refs) - 2) // 2
    sources, targets, sems = refs[1 : count + 1], refs[count + 1 : -1], refs[-1]
    copies = []
    for i, (source, target) in enumerate(zip(sources, targets)):
        rows = source.shape[0] // LOADS
        for j in range(LOADS):
            part = pl.ds(j * rows, rows)
            copies.append(
                pltpu.make_async_copy(source.at[part], target.at[part], sems.at[i * LOADS + j])
            )
    for copy in copies:
        copy.start()
    for copy in copies:
        copy.wait()


def pair_kernel(own_ref, came_ref, out_ref):
    both = jnp.concatenate([own_ref[...].astype(F32), came_ref[...].astype(F32)], axis=0)
    out_ref[...] = both.astype(BF16)


def load(after, *arrays):
    return call(
        load_kernel,
        [jax.ShapeDtypeStruct(a.shape, a.dtype) for a in arrays],
        after,
        *arrays,
        scratch=[pltpu.SemaphoreType.DMA((LOADS * len(arrays),))],
        here=range(1, len(arrays) + 1),
        cost=sum(2 * a.size * a.dtype.itemsize for a in arrays),
        room=50 * MIB,
    )


def plan_kernel(flight, routes_hbm, weights_hbm, out_ref, routes_ref, weights_ref, sems):
    steps, _, rows = routes_ref.shape
    copies = [
        pltpu.make_async_copy(routes_hbm, routes_ref, sems.at[0]),
        pltpu.make_async_copy(weights_hbm, weights_ref, sems.at[1]),
    ]
    for copy in copies:
        copy.start()
    for copy in copies:
        copy.wait()
    lane = lax.broadcasted_iota(jnp.int32, (4 * 2 * PACK, rows), 0)
    block, place = lane // (2 * PACK), lane % PACK
    rest = jnp.where(place == SLOTS, block - 1, jnp.where(place == SLOTS + 1, PIECES + block - 1, -1))
    wanted = jnp.where(block == 0, jnp.where(place < SLOTS, place, -1), rest)
    for s in range(steps):
        routes, scale = routes_ref[s], weights_ref[s]
        for k in range(flight):
            member, slot = slots_of(routes, k, s)
            take = (member & (slot == wanted)).astype(F32)
            weight = jnp.sum(jnp.where(routes == k, scale, 0.0), axis=0, keepdims=True)
            both = jnp.concatenate([take, jnp.broadcast_to(weight, take.shape)], axis=0)
            out_ref[k, s * rows : (s + 1) * rows, :] = both.T


def gate_up_kernel(own_ref, far_ref, *refs):
    quad_refs, (gate_ref, up_ref, out_ref) = refs[:-3], refs[-3:]
    packed = own_ref.shape[1]
    piece = packed // PIECES
    hidden = gate_ref.shape[1]
    pair = jnp.concatenate([own_ref[...].astype(F32), far_ref[...].astype(F32)], axis=0)
    x = jnp.concatenate([pair.astype(BF16)] + [r[...] for r in quad_refs], axis=0)
    rows = x.shape[0]
    tall = jnp.concatenate([x[:, t * piece : (t + 1) * piece] for t in range(PIECES)], axis=0)
    place = lax.broadcasted_iota(jnp.int32, (rows, hidden), 0) % PACK
    for h, ref in enumerate((gate_ref, up_ref)):
        total = dot(x, ref[:packed, :])
        last = dot(tall, ref[packed:, :])
        for t in range(PIECES):
            part = last[t * rows : (t + 1) * rows]
            low = pltpu.roll(part, rows - (SLOTS - t), 0)
            high = pltpu.roll(part, rows - (SLOTS + 1 - PIECES - t), 0)
            total = total + jnp.where(place == t, low, 0.0) + jnp.where(place == PIECES + t, high, 0.0)
        out_ref[:, h * hidden : (h + 1) * hidden] = total


def down_kernel(mine_ref, peer_ref, down_ref, *out_refs):
    rows = mine_ref.shape[0]
    depth = down_ref.shape[0]
    piece = down_ref.shape[1] // (PIECES + 1)
    total = mine_ref[...] + peer_ref[...]
    gate, up = total[:, :depth], total[:, depth:]
    hidden = (gate / (1.0 + jnp.exp(-gate)) * up).astype(BF16).astype(F32)
    place = lax.broadcasted_iota(jnp.int32, (rows, depth), 0) % PACK
    main = jnp.where(place < SLOTS, hidden, 0.0).astype(BF16)
    tall = jnp.concatenate(
        [
            jnp.where(place == SLOTS, pltpu.roll(hidden, SLOTS - t, 0), 0.0)
            + jnp.where(place == SLOTS + 1, pltpu.roll(hidden, SLOTS + 1 - PIECES - t, 0), 0.0)
            for t in range(PIECES)
        ],
        axis=0,
    ).astype(BF16)
    last = dot(tall, down_ref[:, PIECES * piece :])
    count = rows // len(out_refs)
    for t in range(PIECES):
        cols = slice(t * piece, (t + 1) * piece)
        part = (dot(main, down_ref[:, cols]) + last[t * rows : (t + 1) * rows]).astype(BF16)
        for b, ref in enumerate(out_refs):
            ref[:, cols] = part[b * count : (b + 1) * count]


def sum_kernel(first_ref, *refs):
    other_refs, (kept_ref, away_ref) = refs[:-2], refs[-2:]
    total = first_ref[...].astype(F32)
    for ref in other_refs:
        total = total + ref[...].astype(F32)
    kept_ref[...] = total[: kept_ref.shape[0]]
    away_ref[...] = total[kept_ref.shape[0] :].astype(BF16)


def mix_kernel(flight, kept_ref, came_ref, plan_ref, out_ref, held, sems):
    packed = kept_ref.shape[1]
    piece = packed // PIECES
    value = kept_ref[...] + came_ref[...].astype(F32)
    upper = value.astype(BF16).astype(F32)
    lower = value - upper
    total = [None] * (PIECES + 1)
    for k in range(flight):
        weight = plan_ref[k, :, 4 * 2 * PACK : 4 * 2 * PACK + 1]
        main = plan_ref[k, :, : 2 * PACK].astype(BF16)
        rest = plan_ref[k, :, 2 * PACK : 4 * 2 * PACK].astype(BF16)
        take = slice(k * PACK, (k + 1) * PACK)
        both = jnp.concatenate([upper[take], lower[take]], axis=0).astype(BF16)
        tall = jnp.concatenate(
            [both[:, t * piece : (t + 1) * piece] for t in range(PIECES)], axis=0
        )
        for t in range(PIECES + 1):
            if t < PIECES:
                one = weight * dot(main, both[:, t * piece : (t + 1) * piece])
            else:
                one = weight * dot(rest, tall)
            total[t] = one if total[t] is None else total[t] + one
    copies = []
    for t in range(PIECES + 1):
        cols = pl.ds(t * piece, piece)
        held[:, t * piece : (t + 1) * piece] = total[t].astype(BF16)
        copies.append(pltpu.make_async_copy(held.at[:, cols], out_ref.at[:, cols], sems.at[t]))
        copies[-1].start()
    for copy in copies:
        copy.wait()


def local(tokens, routes, route_weights, gate_proj, up_proj, down_proj):
    steps, per_step, half = tokens.shape
    hidden_dev = gate_proj.shape[1]
    group = EF // hidden_dev
    devices = lax.axis_size("expert")
    flight = devices // group
    rows = steps * per_step
    packed = half // (PIECES + 1) * PIECES
    shape = jax.ShapeDtypeStruct
    routes = jnp.transpose(routes, (0, 2, 1))
    route_weights = jnp.transpose(route_weights, (0, 2, 1))

    def swap(x, mask):
        return lax.ppermute(x, "expert", [(i, i ^ mask) for i in range(devices)])

    def cross(x, mask):
        perm = [(2 * i + c, 2 * (i ^ mask) + 1 - c) for i in range(devices) for c in range(2)]
        return lax.ppermute(x, ("expert", "attn"), perm)

    def flip(x):
        return lax.ppermute(x, "attn", [(0, 1), (1, 0)])

    def joined(x, y):
        return call(pair_kernel, shape((2 * x.shape[0], packed), BF16), x, y)

    def across(x):
        if flight == 1:
            return x
        places = [[p + group * b for b in range(flight)] for p in range(group)]
        return lax.all_to_all(x, "expert", 0, 0, axis_index_groups=places, tiled=True)

    count = flight * PACK
    sent = call(
        functools.partial(select_kernel, flight),
        [shape((count, packed // SENT), BF16)] * SENT,
        tokens,
        routes,
        scratch=[
            pltpu.VMEM(tokens.shape, BF16),
            pltpu.VMEM(routes.shape, jnp.int32),
            pltpu.SemaphoreType.DMA((steps + 1,)),
        ],
        here=(0, 1),
        room=55169 * 1024,
    )
    sent = across(jnp.concatenate(sent, axis=1))
    plan = call(
        functools.partial(plan_kernel, flight),
        shape((flight, rows, 128), F32),
        routes,
        route_weights,
        scratch=[
            pltpu.VMEM(routes.shape, jnp.int32),
            pltpu.VMEM(route_weights.shape, F32),
            pltpu.SemaphoreType.DMA((2,)),
        ],
        here=(0, 1),
    )
    high = [bit for bit in (group >> n for n in range(1, group.bit_length())) if bit >= 4]
    block = sent
    for bit in high[:-1]:
        block = joined(block, swap(block, bit))
    far = cross(block, high[-1])
    pair = joined(flip(block), far)
    came = [cross(pair, mask) for mask in QUAD]
    gate_proj, up_proj = load(pair, gate_proj, up_proj)
    products = call(
        gate_up_kernel,
        shape((group * count, 2 * hidden_dev), F32),
        block,
        flip(far),
        *came,
        gate_proj,
        up_proj,
    )
    parts = call(down_kernel, [shape(pair.shape, BF16)] * 4, products, flip(products), down_proj)
    back = [cross(part, mask) for part, mask in zip(parts[1:], QUAD)]
    kept, away = call(
        sum_kernel,
        [shape(block.shape, F32), shape(block.shape, BF16)],
        *back[1:],
        flip(parts[0]),
        back[0],
    )
    kept, came_back = flip(kept), cross(away, high[-1])
    for bit in reversed(high[:-1]):
        summed = kept + came_back.astype(F32)
        rows_in = summed.shape[0] // 2
        kept, away = summed[:rows_in], summed[rows_in:].astype(BF16)
        came_back = swap(away, bit)
    if flight > 1:
        kept = across((kept + came_back.astype(F32)).astype(BF16)).astype(F32)
        came_back = jnp.zeros(kept.shape, BF16)
    mixed = call(
        functools.partial(mix_kernel, flight),
        shape((rows, half), BF16),
        kept,
        came_back,
        plan,
        scratch=[pltpu.VMEM((rows, half), BF16), pltpu.SemaphoreType.DMA((PIECES + 1,))],
        out_here=True,
    )
    return mixed.reshape(steps, per_step, half)


def solution(mesh):
    in_specs = (
        P(None, ("groups", "expert"), "attn"),
        P(None, ("groups", "expert"), None),
        P(None, ("groups", "expert"), None),
        P("attn", "expert"),
        P("attn", "expert"),
        P("expert", "attn"),
    )
    out_specs = P(None, ("groups", "expert"), "attn")
    return jax.shard_map(local, mesh=mesh, in_specs=in_specs, out_specs=out_specs, check_vma=False)
```
